256 devices in a mesh: gx: 8 (over y, z_lo), gy: 8 (over x, core), gz: 4 (over z_hi).
Axes of the slice: x: 4, y: 4, z: 8 (z_hi: 4, z_lo: 2; z = z_hi * 2 + z_lo), core: 2. Of those that a mesh axis runs over, the one named last changes fastest.
Arguments:
- tokens: bfloat16 [512, 12288], P(('gx', 'gz'), 'gy'), may hold values from -6 to 6
- w_in: bfloat16 [12288, 49152], P('gy', ('gx', 'gz')), may hold values from -0.0546875 to 0.0546875
- bias: float32 [49152], P(('gx', 'gz')), may hold values from -4 to 4
- grad_act: bfloat16 [512, 49152], P('gy', ('gx', 'gz')), may hold values from -6 to 6
Outputs:
- act: bfloat16 [512, 49152], P('gy', ('gx', 'gz'))
- grad_bias: float32 [49152], P(('gx', 'gz'))
- grad_weight: bfloat16 [12288, 49152], P('gy', ('gx', 'gz'))
- grad_tokens: bfloat16 [512, 12288], P(('gx', 'gz'), 'gy')
The draws below stay inside these ranges and needn't reach their ends.
All inputs are finite; a program needn't handle non-finite values.
Results may differ from the reference program's by a relative error of at most 0.007.
Values may be sent and summed in bfloat16 or wider, within the bound.
No kernel may reach another device: no remote copies, remote signals or barrier semaphores. Data moves between devices by JAX's collectives and lax.ppermute only.
A program may use at most 64 MiB of HBM per device.

```python
import math
import jax
import jax.numpy as jnp
from jax import lax

D = 12288
FF = 49152
TOKENS = 512


def levels(key, shape, split, smallest, largest):
    factor_of = 1.0
    for axis_at, blocks in split:
        heights = jax.random.uniform(jax.random.fold_in(jax.random.fold_in(key, 6), axis_at), (blocks,), jnp.float32, smallest / len(split), largest / len(split))
        factor_of = factor_of * jnp.repeat(jnp.exp(heights), shape[axis_at] // blocks).reshape((-1,) + (1,) * (len(shape) - 1 - axis_at))
    return factor_of


def gaussian(stream_key, dims, deviation, reach, cuts=(), kind=jnp.bfloat16):
    array = deviation * jax.random.normal(stream_key, dims, jnp.float32)
    if cuts:
        array = array * levels(stream_key, dims, cuts, -0.22, 0.18)
    return jnp.clip(array, -reach, reach).astype(kind)


def setup_inputs(seed: int = 0) -> dict:
    splits = jax.random.split(jax.random.key(seed), 5)
    return {
        "tokens": gaussian(splits[0], (TOKENS, D), 1.0, 6.0, ((0, 32), (1, 8))),
        "w_in": gaussian(splits[1], (D, FF), D ** -0.5, 0.0546875, ((0, 8), (1, 32))),
        "bias": gaussian(splits[2], (FF,), 1.0, 4.0, ((0, 32),), jnp.float32),
        "grad_act": gaussian(splits[3], (TOKENS, FF), 1.0, 6.0, ((0, 8), (1, 32))),
    }


def gelu_pair(v):
    coef = math.sqrt(2.0 / math.pi)
    tangent = jnp.tanh(coef * (v + 0.044715 * v * v * v))
    value = 0.5 * v * (1.0 + tangent)
    slope = 0.5 * (1.0 + tangent) + 0.5 * v * (1.0 - tangent * tangent) * coef * (1.0 + 3.0 * 0.044715 * v * v)
    return (value, slope)

def reference(tokens, w_in, bias, grad_act):
    preact = jnp.dot(tokens, w_in, preferred_element_type=jnp.float32) + bias
    value, slope = gelu_pair(preact)
    act = value.astype(jnp.bfloat16)
    grad_pre = (grad_act.astype(jnp.float32) * slope).astype(jnp.bfloat16)
    grad_bias = lax.optimization_barrier(jnp.sum(grad_pre.astype(jnp.float32), axis=0))
    block_cols = math.gcd(FF, 4096)
    block_count = FF // block_cols
    grad_blocks = jnp.transpose(grad_pre.reshape(TOKENS, block_count, block_cols), (1, 0, 2))

    def weight_block(grad_part):
        return jnp.dot(tokens.T, grad_part, preferred_element_type=jnp.float32).astype(jnp.bfloat16)
    weight_parts = lax.map(weight_block, grad_blocks)
    grad_weight = jnp.transpose(weight_parts, (1, 0, 2)).reshape(D, FF)
    grad_tokens = jnp.dot(grad_pre, w_in.T, preferred_element_type=jnp.float32).astype(jnp.bfloat16)
    return (act, grad_bias, grad_weight, grad_tokens)
```

```python
import functools
import math

import jax
import jax.numpy as jnp
from jax import lax
from jax.experimental import pallas as pl
from jax.experimental.pallas import tpu as pltpu
from jax.sharding import PartitionSpec as P

EVEN = ((0, 2, 4, 6),)
ODD = ((1, 3, 5, 7),)
BF = jnp.bfloat16
F32 = jnp.float32
ROW = 16
VMEM = pltpu.VMEM
LIMIT = 48 * 1024 * 1024
PLANE = ("gx", "gz")


def flat(y, z):
    return (y % 4 * 2 + z % 2) * 4 + z % 8 // 2


def by_plane(array, dy, dz):
    pairs = [(flat(y, z), flat(y + dy, z + dz)) for y in range(4) for z in range(8)]
    return lax.ppermute(array, PLANE, pairs)


def by_line(array, dx, flip=0):
    pairs = [(2 * x + c, (x + dx) % 4 * 2 + (c ^ flip)) for x in range(4) for c in range(2)]
    return lax.ppermute(array, "gy", pairs)


def call(body, ins, outs, grid=(), scratch=(), flops=0, moved=0):
    whole = lambda shape: pl.BlockSpec(shape, lambda *_: (0,) * len(shape))
    in_specs = [s if s is not None else whole(a.shape) for a, s in ins]
    out_specs = [s if s is not None else whole(shape) for shape, _, s in outs]
    return pl.pallas_call(
        body,
        grid=grid or (1,),
        in_specs=in_specs,
        out_specs=out_specs,
        out_shape=[jax.ShapeDtypeStruct(shape, kind) for shape, kind, _ in outs],
        scratch_shapes=list(scratch),
        compiler_params=pltpu.CompilerParams(vmem_limit_bytes=LIMIT),
        cost_estimate=pl.CostEstimate(flops=flops, bytes_accessed=moved, transcendentals=0),
    )(*[a for a, _ in ins])


SMEM = pl.BlockSpec(memory_space=pltpu.SMEM)


def project(place, blocks, w_in, tile=512):
    half = blocks[0].shape[0] // 2
    depth, width = w_in.shape
    rows = 8 * half

    def body(place, b0, b1, b2, b3, w, held, keep, give):
        x, c, y, l = (place[i] for i in range(4))

        @pl.when(pl.program_id(0) == 0)
        def _():
            for t, block in enumerate((b0, b1, b2, b3)):
                at = (y + t - x + 4) % 4
                for p in range(2):
                    side = (l + p + c) % 2
                    held[side, at] = block[p * half : (p + 1) * half, :]

        found = jnp.dot(held[...].reshape(rows, depth), w[...], preferred_element_type=F32)
        keep[...] = found[: rows // 2].reshape(keep.shape)
        give[...] = found[rows // 2 :].reshape(give.shape).astype(BF)

    return call(
        body,
        [(place, SMEM)]
        + [(b, None) for b in blocks]
        + [(w_in, pl.BlockSpec((depth, tile), lambda j: (0, j)))],
        [
            ((2, 4, half, depth), BF, None),
            ((4, half, width), F32, pl.BlockSpec((4, half, tile), lambda j: (0, 0, j))),
            ((4, half, width), BF, pl.BlockSpec((4, half, tile), lambda j: (0, 0, j))),
        ],
        grid=(width // tile,),
        flops=2 * rows * depth * width,
        moved=2 * depth * width + 5 * rows * width,
    )


def add_pair(keep, got):
    _, half, width = keep.shape

    def body(keep, got, own, *rest):
        own[...] = keep[0] + got[0].astype(F32)
        for d, out in enumerate(rest, 1):
            out[...] = (keep[d] + got[d].astype(F32)).astype(BF)

    return call(
        body,
        [(keep, None), (got, None)],
        [((half, width), F32, None)] + [((half, width), BF, None)] * 3,
        flops=keep.size,
        moved=8 * keep.size,
    )


def bend(place, own, parts, bias, grad_act, even, odd):
    half, width = own.shape
    coef = math.sqrt(2.0 / math.pi)

    def body(place, own, p1, p2, p3, bias, grad_act, act, grad):
        c, l, h = place[1], place[3], place[4]
        odd_turn = (c + l) % 2
        for j in range(half // ROW):
            here = slice(j * ROW, (j + 1) * ROW)
            step = jnp.where(odd_turn == 1, odd[j], even[j])
            at = (2 * h + l + step) % 8 // 2
            v = own[here, :] + p1[here, :].astype(F32)
            v = v + (p2[here, :].astype(F32) + p3[here, :].astype(F32)) + bias[...]
            t = jnp.tanh(coef * (v + 0.044715 * v * v * v))
            act[here, :] = (0.5 * v * (1.0 + t)).astype(BF)
            slope = 0.5 * (1.0 + t) + 0.5 * v * (1.0 - t * t) * coef * (1.0 + 3.0 * 0.044715 * v * v)
            grad[here, :] = (grad_act[at].astype(F32) * slope).astype(BF)

    return call(
        body,
        [(place, SMEM), (own, None)] + [(p, None) for p in parts] + [(bias, None), (grad_act, None)],
        [((half, width), BF, None)] * 2,
        flops=30 * own.size,
        moved=14 * own.size,
    )


def back(place, mine, other, w_in, tile=512):
    _, half, width = mine.shape
    depth = w_in.shape[0]
    rows = 8 * half

    def body(place, mine, other, w, o0, o1, o2, o3, found):
        x, c, y, l = (place[i] for i in range(4))
        turn = (((1,), (1,)), ((), ()))
        for side, part in enumerate((mine, other)):
            part = part[...].reshape(4 * half, width)
            product = lax.dot_general(part, w[...], turn, preferred_element_type=F32)
            found[side] = product.reshape(4, half, tile)
        for t, out in enumerate((o0, o1, o2, o3)):
            at = (y + t - x + 4) % 4
            for p in range(2):
                side = (l + p + c) % 2
                out[p * half : (p + 1) * half, :] = found[side, at].astype(out.dtype)

    return call(
        body,
        [(place, SMEM), (mine, None), (other, None)]
        + [(w_in, pl.BlockSpec((tile, width), lambda j: (j, 0)))],
        [
            ((2 * half, depth), F32 if t == 0 else BF, pl.BlockSpec((2 * half, tile), lambda j: (0, j)))
            for t in range(4)
        ],
        grid=(depth // tile,),
        scratch=[VMEM((2, 4, half, tile), F32)],
        flops=2 * rows * depth * width,
        moved=2 * depth * width + 4 * rows * width,
    )


def add_four(own, parts, steps):
    rows, width = own.shape

    def body(own, p1, p2, p3, *outs):
        for j, out in enumerate(outs):
            here = slice(j * ROW, (j + 1) * ROW)
            v = own[here, :] + p1[here, :].astype(F32)
            v = v + (p2[here, :].astype(F32) + p3[here, :].astype(F32))
            out[...] = v.astype(out.dtype)

    return call(
        body,
        [(own, None)] + [(p, None) for p in parts],
        [((ROW, width), F32 if s == 0 else BF, None) for s in steps],
        flops=3 * own.size,
        moved=12 * own.size,
    )


def add_all(arrays):
    def body(*refs):
        total = refs[0][...].astype(F32)
        for ref in refs[1:-1]:
            total = total + ref[...].astype(F32)
        refs[-1][...] = total.astype(BF)

    shape = arrays[0].shape
    return call(
        body,
        [(a, None) for a in arrays],
        [(shape, BF, None)],
        flops=8 * arrays[0].size,
        moved=18 * arrays[0].size,
    )[0]


def weigh(place, held, mine, other, acts, tile=256):
    chunks = len(held)
    half, depth = held[0].shape[2:]
    width = mine[0].shape[2]
    rows = 4 * half

    def body(place, *refs):
        held, refs = refs[:chunks], refs[chunks:]
        mine, refs = refs[:chunks], refs[chunks:]
        other, refs = refs[:chunks], refs[chunks:]
        acts, refs = refs[:chunks], refs[chunks:]
        weight, bias, act = refs

        @pl.when(pl.program_id(0) == 0)
        def _():
            total = jnp.zeros((1, width), F32)
            for ref in mine + other:
                part = ref[...].reshape(rows, width).astype(F32)
                total = total + jnp.sum(part, axis=0, keepdims=True)
            bias[...] = total
            c, l, h = place[1], place[3], place[4]
            odd_turn = (c + l) % 2
            for k in range(chunks):
                for j in range(half // ROW):
                    step = jnp.where(odd_turn == 1, ODD[k][j], EVEN[k][j])
                    at = (2 * h + l + step) % 8 // 2
                    act[at] = acts[k][j * ROW : (j + 1) * ROW, :]

        total = None
        for k in range(chunks):
            for side, part in enumerate((mine[k], other[k])):
                product = lax.dot_general(
                    held[k][side].reshape(rows, tile),
                    part[...].reshape(rows, width),
                    (((0,), (0,)), ((), ())),
                    preferred_element_type=F32,
                )
                total = product if total is None else total + product
        weight[...] = total.astype(BF)

    return call(
        body,
        [(place, SMEM)]
        + [(a, pl.BlockSpec((2, 4, half, tile), lambda j: (0, 0, 0, j))) for a in held]
        + [(a, None) for a in (*mine, *other, *acts)],
        [
            ((depth, width), BF, pl.BlockSpec((tile, width), lambda j: (j, 0))),
            ((1, width), F32, None),
            ((4, ROW, width), BF, None),
        ],
        grid=(depth // tile,),
        flops=4 * chunks * rows * depth * width,
        moved=2 * depth * width + 8 * chunks * rows * width,
    )


def on_device(tokens, w_in, bias, grad_act):
    gx, gy, gz = (lax.axis_index(a) for a in ("gx", "gy", "gz"))
    place = jnp.stack([gy // 2, gy % 2, gx // 2, gx % 2, gz]).astype(jnp.int32)
    width = w_in.shape[1]
    bias = bias.reshape(1, width)
    grad_act = grad_act.reshape(4, ROW, width)
    chunks = range(len(EVEN))

    with jax.named_scope("gather_z"):
        far = {0: tokens}
        for k in chunks:
            for s in EVEN[k] + ODD[k]:
                if s:
                    far[s] = by_plane(tokens, 0, -s)
    blocks = []
    for k in chunks:
        with jax.named_scope("gather_y"):
            own = jnp.concatenate([far[s] for s in EVEN[k] + ODD[k]], axis=0)
            blocks.append([own] + [by_plane(own, -t, 0) for t in (1, 2, 3)])
    held, acts, mine, other, ends = [], [], [], [], {}
    for k in chunks:
        with jax.named_scope("project"):
            order, keep, give = project(place, blocks[k], w_in)
            held.append(order)
        with jax.named_scope("reduce_x"):
            own, *parts = add_pair(keep, by_line(give, 0, 1))
            parts = [by_line(p, d) for d, p in enumerate(parts, 1)]
        with jax.named_scope("bend"):
            act, grad = bend(place, own, parts, bias, grad_act, EVEN[k], ODD[k])
            acts.append(act)
        with jax.named_scope("gather_x"):
            grads = jnp.stack([grad] + [by_line(grad, -d) for d in (1, 2, 3)])
            mine.append(grads)
            other.append(by_line(grads, 0, 1))
    for k in chunks:
        with jax.named_scope("back"):
            own, *parts = back(place, mine[k], other[k], w_in)
        with jax.named_scope("reduce_y"):
            parts = [by_plane(p, t, 0) for t, p in enumerate(parts, 1)]
            steps = EVEN[k] + ODD[k]
            sums = add_four(own, parts, steps)
        with jax.named_scope("reduce_z"):
            for s, part in zip(steps, sums):
                ends[s] = by_plane(part, 0, s) if s else part
    with jax.named_scope("weigh"):
        grad_weight, grad_bias, act = weigh(place, held, mine, other, acts)
    with jax.named_scope("finish"):
        grad_tokens = add_all([ends[s] for s in range(8)])
    return (act.reshape(4 * ROW, width), grad_bias.reshape(width), grad_weight, grad_tokens)


def solution(mesh):
    placed = (P(("gx", "gz"), "gy"), P("gy", ("gx", "gz")), P(("gx", "gz")), P("gy", ("gx", "gz")))
    return jax.shard_map(
        on_device,
        mesh=mesh,
        in_specs=placed,
        out_specs=(
            P("gy", ("gx", "gz")),
            P(("gx", "gz")),
            P("gy", ("gx", "gz")),
            P(("gx", "gz"), "gy"),
        ),
        check_vma=False,
    )
```

```python
import math

import jax
import jax.numpy as jnp
from jax import lax
from jax.experimental import pallas as pl
from jax.experimental.pallas import tpu as pltpu
from jax.sharding import PartitionSpec as P

CHUNKS = ((0, 2), (1, 3))
BF = jnp.bfloat16
F32 = jnp.float32
ROW = 16
LIMIT = 24 * 1024 * 1024
PLANE = ("gx", "gz")
FAST = pl.BlockSpec(memory_space=pltpu.VMEM)
SMEM = pl.BlockSpec(memory_space=pltpu.SMEM)
ANY = pl.BlockSpec(memory_space=pl.ANY)


def by_plane(array, dy, dh, flip=0):
    flat = lambda y, h, l: (y % 4 * 2 + l) * 4 + h % 4
    pairs = [
        (flat(y, h, l), flat(y + dy, h + dh, l ^ flip)) for y in range(4) for h in range(4) for l in range(2)
    ]
    return lax.ppermute(array, PLANE, pairs)


def by_line(array, dx, flip=0):
    pairs = [(2 * x + c, (x + dx) % 4 * 2 + (c ^ flip)) for x in range(4) for c in range(2)]
    return lax.ppermute(array, "gy", pairs)


def call(body, ins, outs, scratch=(), flops=0, moved=0, place=None, grid=(), out_specs=None, after=(), sources=()):
    in_specs = [FAST] * len(ins)
    if place is not None:
        ins, in_specs = [place, *ins], [SMEM, *in_specs]
    ins, in_specs = [*ins, *sources], [*in_specs, *[ANY] * len(sources)]
    used = len(ins)
    ins, in_specs = [*ins, *after], [*in_specs, *[ANY] * len(after)]

    def run(*refs):
        body(*refs[:used], *refs[used + len(after) :])

    return pl.pallas_call(
        run,
        grid=grid,
        in_specs=in_specs,
        out_specs=out_specs or [FAST] * len(outs),
        out_shape=[o if isinstance(o, pl.MemoryRef) else jax.ShapeDtypeStruct(*o) for o in outs],
        scratch_shapes=list(scratch),
        compiler_params=pltpu.CompilerParams(vmem_limit_bytes=LIMIT),
        cost_estimate=pl.CostEstimate(flops=flops, bytes_accessed=moved, transcendentals=0),
    )(*ins)


def fetch(arrays, after):
    def body(*refs):
        ins, outs, done = refs[: len(arrays)], refs[len(arrays) : -1], refs[-1]
        copies = [pltpu.make_async_copy(a, b, done.at[i]) for i, (a, b) in enumerate(zip(ins, outs))]
        for copy in copies:
            copy.start()
        for copy in copies:
            copy.wait()

    return call(
        body,
        [],
        [pltpu.VMEM(a.shape, a.dtype) for a in arrays],
        scratch=[pltpu.SemaphoreType.DMA((len(arrays),))],
        moved=sum(2 * a.size * a.dtype.itemsize for a in arrays),
        sources=[pltpu.with_memory_space_constraint(a, pltpu.HBM) for a in arrays],
        after=after,
    )


def bundle(parts, after=()):
    count = sum(math.prod(p.shape[:-2]) for p in parts)
    width = parts[0].shape[-1]

    def body(*refs):
        at = 0
        for ref in refs[:-1]:
            size = math.prod(ref.shape[:-2])
            refs[-1][at : at + size] = ref[...].reshape(size, ROW, width)
            at += size

    return call(
        body, list(parts), [((count, ROW, width), BF)], moved=4 * count * ROW * width, after=after
    )[0]


def project(place, blocks, w_in, tile=512):
    count = blocks[0].shape[0]
    depth, width = w_in.shape
    rows = 8 * count * ROW

    def body(place, b0, b1, b2, b3, w, held, keep, give):
        x, c, y, l = (place[i] for i in range(4))
        for t, block in enumerate((b0, b1, b2, b3)):
            at = (y + t - x + 4) % 4
            for p in range(2):
                side = (l + p + c) % 2
                for e in range(count):
                    held[side, at, e] = block[e, p]
        for j in range(width // tile):
            cut = slice(j * tile, (j + 1) * tile)
            found = jnp.dot(held[...].reshape(rows, depth), w[:, cut], preferred_element_type=F32)
            keep[:, :, cut] = found[: rows // 2].reshape(4, count * ROW, tile)
            give[:, :, cut] = found[rows // 2 :].reshape(4, count * ROW, tile).astype(BF)

    return call(
        body,
        [*blocks, w_in],
        [
            ((2, 4, count, ROW, depth), BF),
            ((4, count * ROW, width), F32),
            ((4, count * ROW, width), BF),
        ],
        flops=2 * rows * depth * width,
        moved=2 * depth * width + 5 * rows * width,
        place=place,
    )


def add_pair(keep, got):
    _, half, width = keep.shape

    def body(keep, got, own, *rest):
        own[...] = keep[0] + got[0].astype(F32)
        for d, out in enumerate(rest, 1):
            out[...] = (keep[d] + got[d].astype(F32)).astype(BF)

    return call(
        body,
        [keep, got],
        [((half, width), F32)] + [((half, width), BF)] * 3,
        flops=keep.size,
        moved=8 * keep.size,
    )


def bend(place, own, parts, bias, grad_act, chunk):
    half, width = own.shape
    coef = math.sqrt(2.0 / math.pi)

    def body(place, own, p1, p2, p3, bias, grad_act, act, grad):
        for j, e in enumerate(chunk):
            here = slice(j * ROW, (j + 1) * ROW)
            at = (place[4] + e) % 4
            v = own[here, :] + p1[here, :].astype(F32)
            v = v + (p2[here, :].astype(F32) + p3[here, :].astype(F32)) + bias[...]
            t = jnp.tanh(coef * (v + 0.044715 * v * v * v))
            act[here, :] = (0.5 * v * (1.0 + t)).astype(BF)
            slope = 0.5 * (1.0 + t) + 0.5 * v * (1.0 - t * t) * coef * (1.0 + 3.0 * 0.044715 * v * v)
            grad[here, :] = (grad_act[at].astype(F32) * slope).astype(BF)

    return call(
        body,
        [own, *parts, bias, grad_act],
        [((half, width), BF)] * 2,
        flops=30 * own.size,
        moved=14 * own.size,
        place=place,
    )


def back(place, mine, other, w_in, tile=512):
    _, half, width = mine.shape
    count = half // ROW
    depth = w_in.shape[0]
    rows = 8 * half

    def body(place, mine, other, w, o0, o1, o2, o3, all_rows, found):
        x, c, y, l = (place[i] for i in range(4))
        all_rows[: rows // 2] = mine[...].reshape(rows // 2, width)
        all_rows[rows // 2 :] = other[...].reshape(rows // 2, width)
        turn = (((1,), (1,)), ((), ()))
        for j in range(depth // tile):
            cut = slice(j * tile, (j + 1) * tile)
            product = lax.dot_general(all_rows[...], w[cut, :], turn, preferred_element_type=F32)
            found[...] = product.reshape(2, 4, count, ROW, tile)
            for t, out in enumerate((o0, o1, o2, o3)):
                at = (y + t - x + 4) % 4
                for p in range(2):
                    side = (l + p + c) % 2
                    for e in range(count):
                        out[e, p, :, cut] = found[side, at, e].astype(out.dtype)

    return call(
        body,
        [mine, other, w_in],
        [((count, 2, ROW, depth), F32 if t == 0 else BF) for t in range(4)],
        scratch=[pltpu.VMEM((rows, width), BF), pltpu.VMEM((2, 4, count, ROW, tile), F32)],
        flops=2 * rows * depth * width,
        moved=2 * depth * width + 4 * rows * width,
        place=place,
    )


def add_four(own, parts, chunk, after):
    _, _, _, width = own.shape

    def body(own, p1, p2, p3, *outs):
        for j, out in enumerate(outs):
            v = own[j] + p1[j].astype(F32)
            v = v + (p2[j].astype(F32) + p3[j].astype(F32))
            out[...] = v.astype(out.dtype)

    return call(
        body,
        [own, *parts],
        [((2, ROW, width), BF if e else F32) for e in chunk],
        flops=3 * own.size,
        moved=12 * own.size,
        after=after,
    )


def add_rest(arrays):
    width = arrays[0].shape[2]

    def body(*refs):
        total = refs[0][...].astype(F32)
        for ref in refs[1:-2]:
            total = total + ref[...].astype(F32)
        refs[-2][...] = total[0]
        refs[-1][...] = total[1].astype(BF)

    return call(
        body,
        list(arrays),
        [((ROW, width), F32), ((ROW, width), BF)],
        flops=8 * ROW * width,
        moved=18 * ROW * width,
    )


def add_last(own, got):
    def body(own, got, out):
        out[...] = (own[...] + got[...].astype(F32)).astype(BF)

    return call(body, [own, got], [(own.shape, BF)], flops=own.size, moved=8 * own.size)[0]


def settle(place, grads, acts, after):
    width = grads[0].shape[2]

    def body(place, *refs):
        total = jnp.zeros((1, width), F32)
        for ref in refs[: len(grads)]:
            part = ref[...].reshape(-1, width).astype(F32)
            total = total + jnp.sum(part, axis=0, keepdims=True)
        bias, act = refs[-2:]
        bias[...] = total
        for chunk, ref in zip(CHUNKS, refs[len(grads) : -2]):
            for j, e in enumerate(chunk):
                act[(place[4] + e) % 4] = ref[j * ROW : (j + 1) * ROW, :]

    return call(
        body,
        [*grads, *acts],
        [((1, width), F32), ((4, ROW, width), BF)],
        flops=512 * width,
        moved=1024 * width,
        place=place,
        after=after,
    )


def weigh(held, grads, after, tile=512):
    depth = held[0].shape[-1]
    width = grads[0].shape[-1]
    rows = 32 * ROW

    def body(*refs):
        sources, (weight, done, left, right) = refs[:-4], refs[-4:]

        @pl.when(pl.program_id(0) == 0)
        def _():
            done[...] = jnp.zeros_like(done)
            for into, parts in ((left, sources[: len(held)]), (right, sources[len(held) :])):
                at = 0
                for part in parts:
                    size = math.prod(part.shape[:-1])
                    into[at : at + size] = part[...].reshape(size, part.shape[-1])
                    at += size

        cut = pl.ds(pl.multiple_of(pl.program_id(0) * tile, tile), tile)
        weight[...] = lax.dot_general(
            left[:, cut], right[...], (((0,), (0,)), ((), ())), preferred_element_type=F32
        ).astype(BF)

    return call(
        body,
        [*held, *grads],
        [((depth, width), BF), ((8, 128), F32)],
        scratch=[pltpu.VMEM((rows, depth), BF), pltpu.VMEM((rows, width), BF)],
        flops=2 * rows * depth * width,
        moved=2 * depth * width + 4 * rows * width,
        grid=(depth // tile,),
        out_specs=[pl.BlockSpec((tile, width), lambda j: (j, 0)), pl.BlockSpec((8, 128), lambda j: (0, 0))],
        after=after,
    )


def on_device(tokens, w_in, bias, grad_act):
    gx, gy, gz = (lax.axis_index(a) for a in ("gx", "gy", "gz"))
    place = jnp.stack([gy // 2, gy % 2, gx // 2, gx % 2, gz]).astype(jnp.int32)
    width = w_in.shape[1]
    bias = bias.reshape(1, width)
    grad_act = grad_act.reshape(4, ROW, width)

    with jax.named_scope("gather_z"):
        flipped = by_plane(tokens, 0, 0, 1)
        far = [by_plane(tokens, 0, -2), by_plane(tokens, 0, -2, 1)]
        w_in, local = fetch([w_in, tokens], [place])
        first = bundle([local, flipped, *far])
        pair = first[:2]
    blocks = []
    for k, chunk in enumerate(CHUNKS):
        with jax.named_scope("gather_z"):
            if k:
                first = bundle([by_plane(pair, 0, -e) for e in chunk], after=[blocks[0][1], blocks[0][3]])
            own = first.reshape(2, 2, ROW, tokens.shape[1])
        with jax.named_scope("gather_y"):
            blocks.append([own] + [by_plane(own, -t, 0) for t in (1, 2, 3)])
    held, acts, grads, ends = [], [], [], {}
    for chunk, block in zip(CHUNKS, blocks):
        with jax.named_scope("project"):
            order, keep, give = project(place, block, w_in)
            held.append(order)
        with jax.named_scope("reduce_x"):
            own, *parts = add_pair(keep, by_line(give, 0, 1))
            parts = [by_line(p, d) for d, p in enumerate(parts, 1)]
        with jax.named_scope("bend"):
            act, grad = bend(place, own, parts, bias, grad_act, chunk)
            acts.append(act)
        with jax.named_scope("gather_x"):
            mine = jnp.stack([grad] + [by_line(grad, -d) for d in (1, 2, 3)])
            grads += [mine, by_line(mine, 0, 1)]
    partials = []
    for k, chunk in enumerate(CHUNKS):
        with jax.named_scope("back"):
            own, *parts = back(place, *grads[2 * k : 2 * k + 2], w_in)
        with jax.named_scope("reduce_y"):
            partials.append([own] + [by_plane(p, t, 0) for t, p in enumerate(parts, 1)])
    with jax.named_scope("settle"):
        grad_bias, act = settle(place, grads, acts, [partials[1][0]])
    with jax.named_scope("weigh"):
        grad_weight, weighed = weigh(held, grads, [partials[1][0]])
    for (own, *parts), chunk, beside in zip(partials, CHUNKS, (grad_bias, weighed)):
        with jax.named_scope("reduce_y"):
            sums = add_four(own, parts, chunk, [beside])
        with jax.named_scope("reduce_z"):
            for e, part in zip(chunk, sums):
                ends[e] = by_plane(part, 0, e) if e else part
    with jax.named_scope("reduce_z"):
        own, part = add_rest([ends[e] for e in range(4)])
        part = by_plane(part, 0, 0, 1)
    with jax.named_scope("finish"):
        grad_tokens = add_last(own, part)
    return (act.reshape(4 * ROW, width), grad_bias.reshape(width), grad_weight, grad_tokens)


def solution(mesh):
    placed = (P(("gx", "gz"), "gy"), P("gy", ("gx", "gz")), P(("gx", "gz")), P("gy", ("gx", "gz")))
    return jax.shard_map(
        on_device,
        mesh=mesh,
        in_specs=placed,
        out_specs=(
            P("gy", ("gx", "gz")),
            P(("gx", "gz")),
            P("gy", ("gx", "gz")),
            P(("gx", "gz"), "gy"),
        ),
        check_vma=False,
    )
```

```python
import math

import jax
import jax.numpy as jnp
from jax import lax
from jax.experimental import pallas as pl
from jax.experimental.pallas import tpu as pltpu
from jax.sharding import PartitionSpec as P

CHUNKS = ((0, 2), (1, 3))
BF = jnp.bfloat16
F32 = jnp.float32
ROW = 16
LIMIT = 24 * 1024 * 1024
PLANE = ("gx", "gz")
FAST = pl.BlockSpec(memory_space=pltpu.VMEM)
SMEM = pl.BlockSpec(memory_space=pltpu.SMEM)
ANY = pl.BlockSpec(memory_space=pl.ANY)


def by_plane(array, dy, dh, flip=0):
    flat = lambda y, h, l: (y % 4 * 2 + l) * 4 + h % 4
    pairs = [
        (flat(y, h, l), flat(y + dy, h + dh, l ^ flip)) for y in range(4) for h in range(4) for l in range(2)
    ]
    return lax.ppermute(array, PLANE, pairs)


def by_line(array, dx, flip=0):
    pairs = [(2 * x + c, (x + dx) % 4 * 2 + (c ^ flip)) for x in range(4) for c in range(2)]
    return lax.ppermute(array, "gy", pairs)


def call(body, ins, outs, scratch=(), flops=0, moved=0, place=None, grid=(), out_specs=None, after=(), sources=()):
    in_specs = [FAST] * len(ins)
    if place is not None:
        ins, in_specs = [place, *ins], [SMEM, *in_specs]
    ins, in_specs = [*ins, *sources], [*in_specs, *[ANY] * len(sources)]
    used = len(ins)
    ins, in_specs = [*ins, *after], [*in_specs, *[ANY] * len(after)]

    def run(*refs):
        body(*refs[:used], *refs[used + len(after) :])

    return pl.pallas_call(
        run,
        grid=grid,
        in_specs=in_specs,
        out_specs=out_specs or [FAST] * len(outs),
        out_shape=[o if isinstance(o, pl.MemoryRef) else jax.ShapeDtypeStruct(*o) for o in outs],
        scratch_shapes=list(scratch),
        compiler_params=pltpu.CompilerParams(vmem_limit_bytes=LIMIT),
        cost_estimate=pl.CostEstimate(flops=0, bytes_accessed=0, transcendentals=0),
    )(*ins)


def fetch(arrays, after):
    def body(*refs):
        ins, outs, done = refs[: len(arrays)], refs[len(arrays) : -1], refs[-1]
        copies = [pltpu.make_async_copy(a, b, done.at[i]) for i, (a, b) in enumerate(zip(ins, outs))]
        for copy in copies:
            copy.start()
        for copy in copies:
            copy.wait()

    return call(
        body,
        [],
        [pltpu.VMEM(a.shape, a.dtype) for a in arrays],
        scratch=[pltpu.SemaphoreType.DMA((len(arrays),))],
        moved=sum(2 * a.size * a.dtype.itemsize for a in arrays),
        sources=[pltpu.with_memory_space_constraint(a, pltpu.HBM) for a in arrays],
        after=after,
    )


def bundle(parts, after=()):
    count = sum(math.prod(p.shape[:-2]) for p in parts)
    width = parts[0].shape[-1]

    def body(*refs):
        at = 0
        for ref in refs[:-1]:
            size = math.prod(ref.shape[:-2])
            refs[-1][at : at + size] = ref[...].reshape(size, ROW, width)
            at += size

    return call(
        body, list(parts), [((count, ROW, width), BF)], moved=4 * count * ROW * width, after=after
    )[0]


def project(place, blocks, w_in, tile=512):
    count = blocks[0].shape[0]
    depth, width = w_in.shape
    rows = 8 * count * ROW

    def body(place, b0, b1, b2, b3, w, held, keep, give):
        x, c, y, l = (place[i] for i in range(4))
        for t, block in enumerate((b0, b1, b2, b3)):
            at = (y + t - x + 4) & 3
            for p in range(2):
                side = (l + p + c) & 1
                for e in range(count):
                    held[side, at, e] = block[e, p]
        for j in range(width // tile):
            cut = slice(j * tile, (j + 1) * tile)
            found = jnp.dot(held[...].reshape(rows, depth), w[:, cut], preferred_element_type=F32)
            keep[:, :, cut] = found[: rows // 2].reshape(4, count * ROW, tile)
            give[:, :, cut] = found[rows // 2 :].reshape(4, count * ROW, tile).astype(BF)

    return call(
        body,
        [*blocks, w_in],
        [
            ((2, 4, count, ROW, depth), BF),
            ((4, count * ROW, width), F32),
            ((4, count * ROW, width), BF),
        ],
        flops=2 * rows * depth * width,
        moved=2 * depth * width + 5 * rows * width,
        place=place,
    )


def add_pair(keep, got):
    _, half, width = keep.shape

    def body(keep, got, own, *rest):
        own[...] = keep[0] + got[0].astype(F32)
        for d, out in enumerate(rest, 1):
            out[...] = (keep[d] + got[d].astype(F32)).astype(BF)

    return call(
        body,
        [keep, got],
        [((half, width), F32)] + [((half, width), BF)] * 3,
        flops=keep.size,
        moved=8 * keep.size,
    )


def bend(place, own, parts, bias, grad_act, chunk):
    half, width = own.shape
    coef = math.sqrt(2.0 / math.pi)

    def body(place, own, p1, p2, p3, bias, grad_act, act, grad):
        for j, e in enumerate(chunk):
            here = slice(j * ROW, (j + 1) * ROW)
            at = (place[4] + e) & 3
            v = own[here, :] + p1[here, :].astype(F32)
            v = v + (p2[here, :].astype(F32) + p3[here, :].astype(F32)) + bias[...]
            t = jnp.tanh(coef * (v + 0.044715 * v * v * v))
            act[here, :] = (0.5 * v * (1.0 + t)).astype(BF)
            slope = 0.5 * (1.0 + t) + 0.5 * v * (1.0 - t * t) * coef * (1.0 + 3.0 * 0.044715 * v * v)
            grad[here, :] = (grad_act[at].astype(F32) * slope).astype(BF)

    return call(
        body,
        [own, *parts, bias, grad_act],
        [((half, width), BF)] * 2,
        flops=30 * own.size,
        moved=14 * own.size,
        place=place,
    )


def back(place, mine, other, w_in, tile=512):
    _, half, width = mine.shape
    count = half // ROW
    depth = w_in.shape[0]
    rows = 8 * half

    def body(place, mine, other, w, o0, o1, o2, o3, all_rows, found):
        x, c, y, l = (place[i] for i in range(4))
        all_rows[: rows // 2] = mine[...].reshape(rows // 2, width)
        all_rows[rows // 2 :] = other[...].reshape(rows // 2, width)
        turn = (((1,), (1,)), ((), ()))
        for j in range(depth // tile):
            cut = slice(j * tile, (j + 1) * tile)
            product = lax.dot_general(all_rows[...], w[cut, :], turn, preferred_element_type=F32)
            found[...] = product.reshape(2, 4, count, ROW, tile)
            for t, out in enumerate((o0, o1, o2, o3)):
                at = (y + t - x + 4) & 3
                for p in range(2):
                    side = (l + p + c) & 1
                    for e in range(count):
                        out[e, p, :, cut] = found[side, at, e].astype(out.dtype)

    return call(
        body,
        [mine, other, w_in],
        [((count, 2, ROW, depth), F32 if t == 0 else BF) for t in range(4)],
        scratch=[pltpu.VMEM((rows, width), BF), pltpu.VMEM((2, 4, count, ROW, tile), F32)],
        flops=2 * rows * depth * width,
        moved=2 * depth * width + 4 * rows * width,
        place=place,
    )


def add_four(own, parts, chunk, after):
    _, _, _, width = own.shape

    def body(own, p1, p2, p3, *outs):
        for i, out in enumerate(outs):
            j, p = i // 2, i % 2
            v = own[j, p] + p1[j, p].astype(F32)
            v = v + (p2[j, p].astype(F32) + p3[j, p].astype(F32))
            out[...] = v.astype(out.dtype)

    return call(
        body,
        [own, *parts],
        [((ROW, width), BF if e or p else F32) for e in chunk for p in range(2)],
        flops=3 * own.size,
        moved=12 * own.size,
        after=after,
    )


def add_last(arrays, after):
    def body(*refs):
        total = refs[0][...]
        for ref in refs[1:-1]:
            total = total + ref[...].astype(F32)
        refs[-1][...] = total.astype(BF)

    return call(body, arrays, [(arrays[0].shape, BF)], after=after)[0]


def settle(place, grads, acts, after):
    width = grads[0].shape[2]

    def body(place, *refs):
        total = jnp.zeros((1, width), F32)
        for ref in refs[: len(grads)]:
            part = ref[...].reshape(-1, width).astype(F32)
            total = total + jnp.sum(part, axis=0, keepdims=True)
        bias, act = refs[-2:]
        bias[...] = total
        for chunk, ref in zip(CHUNKS, refs[len(grads) : -2]):
            for j, e in enumerate(chunk):
                act[(place[4] + e) & 3] = ref[j * ROW : (j + 1) * ROW, :]

    return call(
        body,
        [*grads, *acts],
        [((1, width), F32), ((4, ROW, width), BF)],
        flops=512 * width,
        moved=1024 * width,
        place=place,
        after=after,
    )


def weigh(held, grads, after, tile=512):
    depth = held[0].shape[-1]
    width = grads[0].shape[-1]
    rows = 32 * ROW

    def body(*refs):
        sources, (weight, done, left, right) = refs[:-4], refs[-4:]

        @pl.when(pl.program_id(0) == 0)
        def _():
            done[...] = jnp.zeros_like(done)
            for into, parts in ((left, sources[: len(held)]), (right, sources[len(held) :])):
                at = 0
                for part in parts:
                    size = math.prod(part.shape[:-1])
                    into[at : at + size] = part[...].reshape(size, part.shape[-1])
                    at += size

        cut = pl.ds(pl.multiple_of(pl.program_id(0) * tile, tile), tile)
        weight[...] = lax.dot_general(
            left[:, cut], right[...], (((0,), (0,)), ((), ())), preferred_element_type=F32
        ).astype(BF)

    return call(
        body,
        [*held, *grads],
        [((depth, width), BF), ((8, 128), F32)],
        scratch=[pltpu.VMEM((rows, depth), BF), pltpu.VMEM((rows, width), BF)],
        flops=2 * rows * depth * width,
        moved=2 * depth * width + 4 * rows * width,
        grid=(depth // tile,),
        out_specs=[pl.BlockSpec((tile, width), lambda j: (j, 0)), pl.BlockSpec((8, 128), lambda j: (0, 0))],
        after=after,
    )


def on_device(tokens, w_in, bias, grad_act):
    gx, gy, gz = (lax.axis_index(a) for a in ("gx", "gy", "gz"))
    place = jnp.stack([gy // 2, gy % 2, gx // 2, gx % 2, gz]).astype(jnp.int32)
    width = w_in.shape[1]
    bias = bias.reshape(1, width)
    grad_act = grad_act.reshape(4, ROW, width)

    with jax.named_scope("gather_z"):
        flipped = by_plane(tokens, 0, 0, 1)
        far = [by_plane(tokens, 0, -2), by_plane(tokens, 0, -2, 1)]
        w_in, local = fetch([w_in, tokens], [place])
        first = bundle([local, flipped, *far])
        pair = first[:2]
    blocks = []
    for k, chunk in enumerate(CHUNKS):
        with jax.named_scope("gather_z"):
            if k:
                first = bundle([by_plane(pair, 0, -e) for e in chunk], after=[blocks[0][1], blocks[0][3]])
            own = first.reshape(2, 2, ROW, tokens.shape[1])
        with jax.named_scope("gather_y"):
            blocks.append([own] + [by_plane(own, -t, 0) for t in (1, 2, 3)])
    held, acts, grads, ends = [], [], [], {}
    for chunk, block in zip(CHUNKS, blocks):
        with jax.named_scope("project"):
            order, keep, give = project(place, block, w_in)
            held.append(order)
        with jax.named_scope("reduce_x"):
            own, *parts = add_pair(keep, by_line(give, 0, 1))
            parts = [by_line(p, d) for d, p in enumerate(parts, 1)]
        with jax.named_scope("bend"):
            act, grad = bend(place, own, parts, bias, grad_act, chunk)
            acts.append(act)
        with jax.named_scope("gather_x"):
            mine = jnp.stack([grad] + [by_line(grad, -d) for d in (1, 2, 3)])
            grads += [mine, by_line(mine, 0, 1)]
    partials = []
    for k, chunk in enumerate(CHUNKS):
        with jax.named_scope("back"):
            own, *parts = back(place, *grads[2 * k : 2 * k + 2], w_in)
        with jax.named_scope("reduce_y"):
            partials.append([own] + [by_plane(p, t, 0) for t, p in enumerate(parts, 1)])
    with jax.named_scope("weigh"):
        grad_weight, weighed = weigh(held, grads, [partials[1][0]])
    for (own, *parts), chunk, beside in zip(partials, CHUNKS, ([weighed], [])):
        with jax.named_scope("reduce_y"):
            sums = add_four(own, parts, chunk, beside)
        with jax.named_scope("reduce_z"):
            for i, part in enumerate(sums):
                e, p = chunk[i // 2], i % 2
                ends[e, p] = by_plane(part, 0, e, p) if e or p else part
    with jax.named_scope("settle"):
        grad_bias, act = settle(place, grads, acts, sums[:1])
    with jax.named_scope("finish"):
        grad_tokens = add_last([ends[e, p] for e in range(4) for p in range(2)], [grad_bias])
    return (act.reshape(4 * ROW, width), grad_bias.reshape(width), grad_weight, grad_tokens)


def solution(mesh):
    placed = (P(("gx", "gz"), "gy"), P("gy", ("gx", "gz")), P(("gx", "gz")), P("gy", ("gx", "gz")))
    return jax.shard_map(
        on_device,
        mesh=mesh,
        in_specs=placed,
        out_specs=(
            P("gy", ("gx", "gz")),
            P(("gx", "gz")),
            P("gy", ("gx", "gz")),
            P(("gx", "gz"), "gy"),
        ),
        check_vma=False,
    )
```

```python
import math

import jax
import jax.numpy as jnp
from jax import lax
from jax.experimental import pallas as pl
from jax.experimental.pallas import tpu as pltpu
from jax.sharding import PartitionSpec as P

CHUNKS = ((0, 2), (1, 3))
BF = jnp.bfloat16
F32 = jnp.float32
ROW = 16
LIMIT = 24 * 1024 * 1024
PLANE = ("gx", "gz")
FAST = pl.BlockSpec(memory_space=pltpu.VMEM)
SMEM = pl.BlockSpec(memory_space=pltpu.SMEM)
ANY = pl.BlockSpec(memory_space=pl.ANY)


def by_plane(array, dy, dh, flip=0):
    flat = lambda y, h, l: (y % 4 * 2 + l) * 4 + h % 4
    pairs = [
        (flat(y, h, l), flat(y + dy, h + dh, l ^ flip)) for y in range(4) for h in range(4) for l in range(2)
    ]
    return lax.ppermute(array, PLANE, pairs)


def by_line(array, dx, flip=0):
    pairs = [(2 * x + c, (x + dx) % 4 * 2 + (c ^ flip)) for x in range(4) for c in range(2)]
    return lax.ppermute(array, "gy", pairs)


def call(body, ins, outs, scratch=(), flops=0, moved=0, place=None, grid=(), out_specs=None, after=(), sources=()):
    in_specs = [FAST] * len(ins)
    if place is not None:
        ins, in_specs = [place, *ins], [SMEM, *in_specs]
    ins, in_specs = [*ins, *sources], [*in_specs, *[ANY] * len(sources)]
    used = len(ins)
    ins, in_specs = [*ins, *after], [*in_specs, *[ANY] * len(after)]

    def run(*refs):
        body(*refs[:used], *refs[used + len(after) :])

    return pl.pallas_call(
        run,
        grid=grid,
        in_specs=in_specs,
        out_specs=out_specs or [FAST] * len(outs),
        out_shape=[o if isinstance(o, pl.MemoryRef) else jax.ShapeDtypeStruct(*o) for o in outs],
        scratch_shapes=list(scratch),
        compiler_params=pltpu.CompilerParams(vmem_limit_bytes=LIMIT),
        cost_estimate=pl.CostEstimate(flops=0, bytes_accessed=0, transcendentals=0),
    )(*ins)


def fetch(arrays, after):
    def body(*refs):
        ins, outs, done = refs[: len(arrays)], refs[len(arrays) : -1], refs[-1]
        copies = [pltpu.make_async_copy(a, b, done.at[i]) for i, (a, b) in enumerate(zip(ins, outs))]
        for copy in copies:
            copy.start()
        for copy in copies:
            copy.wait()

    return call(
        body,
        [],
        [pltpu.VMEM(a.shape, a.dtype) for a in arrays],
        scratch=[pltpu.SemaphoreType.DMA((len(arrays),))],
        moved=sum(2 * a.size * a.dtype.itemsize for a in arrays),
        sources=[pltpu.with_memory_space_constraint(a, pltpu.HBM) for a in arrays],
        after=after,
    )


def bundle(parts, after=()):
    count = sum(math.prod(p.shape[:-2]) for p in parts)
    width = parts[0].shape[-1]

    def body(*refs):
        at = 0
        for ref in refs[:-1]:
            size = math.prod(ref.shape[:-2])
            refs[-1][at : at + size] = ref[...].reshape(size, ROW, width)
            at += size

    return call(
        body, list(parts), [((count, ROW, width), BF)], moved=4 * count * ROW * width, after=after
    )[0]


def project(place, blocks, w_in, tile=512):
    count = blocks[0].shape[0]
    depth, width = w_in.shape
    rows = 8 * count * ROW

    def body(place, b0, b1, b2, b3, w, held, keep, give):
        x, c, y, l = (place[i] for i in range(4))
        for t, block in enumerate((b0, b1, b2, b3)):
            at = (y + t - x + 4) & 3
            for p in range(2):
                side = (l + p + c) & 1
                for e in range(count):
                    held[side, at, e] = block[e, p]
        for j in range(width // tile):
            cut = slice(j * tile, (j + 1) * tile)
            found = jnp.dot(held[...].reshape(rows, depth), w[:, cut], preferred_element_type=F32)
            keep[:, :, cut] = found[: rows // 2].reshape(4, count * ROW, tile)
            give[:, :, cut] = found[rows // 2 :].reshape(4, count * ROW, tile).astype(BF)

    return call(
        body,
        [*blocks, w_in],
        [
            ((2, 4, count, ROW, depth), BF),
            ((4, count * ROW, width), F32),
            ((4, count * ROW, width), BF),
        ],
        flops=2 * rows * depth * width,
        moved=2 * depth * width + 5 * rows * width,
        place=place,
    )


def add_pair(keep, got):
    _, half, width = keep.shape

    def body(keep, got, own, *rest):
        own[...] = keep[0] + got[0].astype(F32)
        for d, out in enumerate(rest, 1):
            out[...] = (keep[d] + got[d].astype(F32)).astype(BF)

    return call(
        body,
        [keep, got],
        [((half, width), F32)] + [((half, width), BF)] * 3,
        flops=keep.size,
        moved=8 * keep.size,
    )


def bend(place, own, parts, bias, grad_act, chunk):
    half, width = own.shape
    coef = math.sqrt(2.0 / math.pi)

    def body(place, own, p1, p2, p3, bias, grad_act, act, grad):
        for j, e in enumerate(chunk):
            here = slice(j * ROW, (j + 1) * ROW)
            at = (place[4] + e) & 3
            v = own[here, :] + p1[here, :].astype(F32)
            v = v + (p2[here, :].astype(F32) + p3[here, :].astype(F32)) + bias[...]
            t = jnp.tanh(coef * (v + 0.044715 * v * v * v))
            act[here, :] = (0.5 * v * (1.0 + t)).astype(BF)
            slope = 0.5 * (1.0 + t) + 0.5 * v * (1.0 - t * t) * coef * (1.0 + 3.0 * 0.044715 * v * v)
            grad[here, :] = (grad_act[at].astype(F32) * slope).astype(BF)

    return call(
        body,
        [own, *parts, bias, grad_act],
        [((half, width), BF)] * 2,
        flops=30 * own.size,
        moved=14 * own.size,
        place=place,
    )


def back(place, mine, other, w_in, tile=512):
    _, half, width = mine.shape
    count = half // ROW
    depth = w_in.shape[0]
    rows = 8 * half

    def body(place, mine, other, w, o0, o1, o2, o3, all_rows, found):
        x, c, y, l = (place[i] for i in range(4))
        all_rows[: rows // 2] = mine[...].reshape(rows // 2, width)
        all_rows[rows // 2 :] = other[...].reshape(rows // 2, width)
        turn = (((1,), (1,)), ((), ()))
        for j in range(depth // tile):
            cut = slice(j * tile, (j + 1) * tile)
            product = lax.dot_general(all_rows[...], w[cut, :], turn, preferred_element_type=F32)
            found[...] = product.reshape(2, 4, count, ROW, tile)
            for t, out in enumerate((o0, o1, o2, o3)):
                at = (y + t - x + 4) & 3
                for p in range(2):
                    side = (l + p + c) & 1
                    for e in range(count):
                        out[e, p, :, cut] = found[side, at, e].astype(out.dtype)

    return call(
        body,
        [mine, other, w_in],
        [((count, 2, ROW, depth), F32 if t == 0 else BF) for t in range(4)],
        scratch=[pltpu.VMEM((rows, width), BF), pltpu.VMEM((2, 4, count, ROW, tile), F32)],
        flops=2 * rows * depth * width,
        moved=2 * depth * width + 4 * rows * width,
        place=place,
    )


def add_four(own, parts, chunk, after):
    _, _, _, width = own.shape

    def body(own, p1, p2, p3, *outs):
        for i, out in enumerate(outs):
            j, p = i // 2, i % 2
            v = own[j, p] + p1[j, p].astype(F32)
            v = v + (p2[j, p].astype(F32) + p3[j, p].astype(F32))
            out[...] = v.astype(out.dtype)

    return call(
        body,
        [own, *parts],
        [((ROW, width), BF if e or p else F32) for e in chunk for p in range(2)],
        flops=3 * own.size,
        moved=12 * own.size,
        after=after,
    )


def add_last(arrays, after):
    def body(*refs):
        total = refs[0][...]
        for ref in refs[1:-1]:
            total = total + ref[...].astype(F32)
        refs[-1][...] = total.astype(BF)

    return call(body, arrays, [(arrays[0].shape, BF)], after=after)[0]


def settle(place, grads, acts, after):
    width = grads[0].shape[2]

    def body(place, *refs):
        rows = jnp.concatenate([ref[...].reshape(-1, width) for ref in refs[: len(grads)]])
        ones = jnp.ones((ROW, rows.shape[0]), BF)
        bias, act = refs[-2:]
        bias[...] = jnp.dot(ones, rows, preferred_element_type=F32)[:1]
        for chunk, ref in zip(CHUNKS, refs[len(grads) : -2]):
            for j, e in enumerate(chunk):
                act[(place[4] + e) & 3] = ref[j * ROW : (j + 1) * ROW, :]

    return call(
        body,
        [*grads, *acts],
        [((1, width), F32), ((4, ROW, width), BF)],
        flops=512 * width,
        moved=1024 * width,
        place=place,
        after=after,
    )


def weigh(held, grads, after, tile=512):
    depth = held[0].shape[-1]
    width = grads[0].shape[-1]
    rows = 32 * ROW

    def body(*refs):
        sources, (weight, done, left, right) = refs[:-4], refs[-4:]

        @pl.when(pl.program_id(0) == 0)
        def _():
            done[...] = jnp.zeros_like(done)
            for into, parts in ((left, sources[: len(held)]), (right, sources[len(held) :])):
                at = 0
                for part in parts:
                    size = math.prod(part.shape[:-1])
                    into[at : at + size] = part[...].reshape(size, part.shape[-1])
                    at += size

        cut = pl.ds(pl.multiple_of(pl.program_id(0) * tile, tile), tile)
        weight[...] = lax.dot_general(
            left[:, cut], right[...], (((0,), (0,)), ((), ())), preferred_element_type=F32
        ).astype(BF)

    return call(
        body,
        [*held, *grads],
        [((depth, width), BF), ((8, 128), F32)],
        scratch=[pltpu.VMEM((rows, depth), BF), pltpu.VMEM((rows, width), BF)],
        flops=2 * rows * depth * width,
        moved=2 * depth * width + 4 * rows * width,
        grid=(depth // tile,),
        out_specs=[pl.BlockSpec((tile, width), lambda j: (j, 0)), pl.BlockSpec((8, 128), lambda j: (0, 0))],
        after=after,
    )


def on_device(tokens, w_in, bias, grad_act):
    gx, gy, gz = (lax.axis_index(a) for a in ("gx", "gy", "gz"))
    place = jnp.stack([gy // 2, gy % 2, gx // 2, gx % 2, gz]).astype(jnp.int32)
    width = w_in.shape[1]
    bias = bias.reshape(1, width)
    grad_act = grad_act.reshape(4, ROW, width)

    with jax.named_scope("gather_z"):
        flipped = by_plane(tokens, 0, 0, 1)
        far = [by_plane(tokens, 0, -2), by_plane(tokens, 0, -2, 1)]
        w_in, local = fetch([w_in, tokens], [place])
        first = bundle([local, flipped, *far])
        pair = first[:2]
    blocks = []
    for k, chunk in enumerate(CHUNKS):
        with jax.named_scope("gather_z"):
            if k:
                first = bundle([by_plane(pair, 0, -e) for e in chunk], after=[blocks[0][1], blocks[0][3]])
            own = first.reshape(2, 2, ROW, tokens.shape[1])
        with jax.named_scope("gather_y"):
            blocks.append([own] + [by_plane(own, -t, 0) for t in (1, 2, 3)])
    held, acts, grads, ends = [], [], [], {}
    for chunk, block in zip(CHUNKS, blocks):
        with jax.named_scope("project"):
            order, keep, give = project(place, block, w_in)
            held.append(order)
        with jax.named_scope("reduce_x"):
            own, *parts = add_pair(keep, by_line(give, 0, 1))
            parts = [by_line(p, d) for d, p in enumerate(parts, 1)]
        with jax.named_scope("bend"):
            act, grad = bend(place, own, parts, bias, grad_act, chunk)
            acts.append(act)
        with jax.named_scope("gather_x"):
            mine = jnp.stack([grad] + [by_line(grad, -d) for d in (1, 2, 3)])
            grads += [mine, by_line(mine, 0, 1)]
    partials = []
    for k, chunk in enumerate(CHUNKS):
        with jax.named_scope("back"):
            own, *parts = back(place, *grads[2 * k : 2 * k + 2], w_in)
        with jax.named_scope("reduce_y"):
            partials.append([own] + [by_plane(p, t, 0) for t, p in enumerate(parts, 1)])
    with jax.named_scope("weigh"):
        grad_weight, weighed = weigh(held, grads, [partials[1][0]])
    for (own, *parts), chunk, beside in zip(partials, CHUNKS, ([weighed], [])):
        with jax.named_scope("reduce_y"):
            sums = add_four(own, parts, chunk, beside)
        with jax.named_scope("reduce_z"):
            for i, part in enumerate(sums):
                e, p = chunk[i // 2], i % 2
                ends[e, p] = by_plane(part, 0, e, p) if e or p else part
    with jax.named_scope("settle"):
        grad_bias, act = settle(place, grads, acts, sums[:1])
    with jax.named_scope("finish"):
        grad_tokens = add_last([ends[e, p] for e in range(4) for p in range(2)], [grad_bias])
    return (act.reshape(4 * ROW, width), grad_bias.reshape(width), grad_weight, grad_tokens)


def solution(mesh):
    placed = (P(("gx", "gz"), "gy"), P("gy", ("gx", "gz")), P(("gx", "gz")), P("gy", ("gx", "gz")))
    return jax.shard_map(
        on_device,
        mesh=mesh,
        in_specs=placed,
        out_specs=(
            P("gy", ("gx", "gz")),
            P(("gx", "gz")),
            P("gy", ("gx", "gz")),
            P(("gx", "gz"), "gy"),
        ),
        check_vma=False,
    )
```
